128 devices in a mesh: row: 8 (over y_hi, x), col: 16 (over z, y_lo, core).
Axes of the slice: x: 4, y: 4 (y_hi: 2, y_lo: 2; y = y_hi * 2 + y_lo), z: 4, core: 2. Of those that a mesh axis runs over, the one named last changes fastest.
Arguments:
- source: float32 [32768, 128], P(('row', 'col')), may hold values from -6 to 6
- value: bfloat16 [32768, 32768], P('row', 'col'), may hold values from -128 to 127, as said below
- occupancy: int32 [256, 256], P('row', 'col'), may hold values 0 or 1
- exponent: int32 [256, 256], P('row', 'col'), may hold values from -3 to 3, as said below
Outputs:
- diffused: float32 [32768, 128], P(('row', 'col'))
The draws below stay inside these ranges and needn't reach their ends.
Inputs may be any that keep to these rules, and one draw needn't show every extreme that they name: `value`: whole numbers, drawn independently; both ends of the range occur. `exponent`: tile exponents; every value of the range occurs.
All inputs are finite; a program needn't handle non-finite values. No bound on the sum of `occupancy` on one device may be relied on, other than what follows from the above.
Results may differ from the reference program's by a relative error of at most 0.0003.
Values sent between devices are 32-bit elements; how exact they have to be, the bound alone decides.
A program may use at most 128 MiB of HBM per device.

```python
import jax
import jax.numpy as jnp
from jax import lax

FEATURES = 128
SPAN = 256
STEPS = 3
BLOCK = 128
NODES = 32768
N_ROW = 8
N_COL = 16


def draw_value(key, part):
    entry_key, pick_key = jax.random.split(jax.random.fold_in(key, 29))
    row_pick, high_col, low_col = jax.random.split(pick_key, 3)
    entries = jax.random.randint(entry_key, (NODES, NODES), -128, 128, dtype=jnp.int32)
    top_row = jax.random.randint(row_pick, (), 0, NODES, dtype=jnp.int32)
    bottom_row = (top_row + 1) % NODES
    top_col = jax.random.randint(high_col, (), 0, NODES, dtype=jnp.int32)
    bottom_col = jax.random.randint(low_col, (), 0, NODES, dtype=jnp.int32)
    row_index = jnp.arange(NODES, dtype=jnp.int32)[:, None]
    col_index = jnp.arange(NODES, dtype=jnp.int32)[None, :]
    entries = jnp.where((row_index == top_row) & (col_index == top_col), jnp.int32(127), entries)
    entries = jnp.where((row_index == bottom_row) & (col_index == bottom_col), jnp.int32(-128), entries)
    return entries.astype(jnp.float32).astype(jnp.bfloat16)


def draw_exponent(key, part):
    nblocks = NODES // BLOCK
    first_key, second_key = jax.random.split(jax.random.fold_in(key, 17))
    row_level = (jax.random.permutation(first_key, nblocks) % 4).astype(jnp.int32)
    offset = jax.random.randint(second_key, (), 0, 2, dtype=jnp.int32)
    columns = jnp.arange(nblocks, dtype=jnp.int32)
    col_level = (columns + offset) % 2
    rising = 3 * columns // nblocks
    return (row_level[:, None] + col_level[None, :] + rising[None, :] - 3).astype(jnp.int32)


def plant(values, key, least, top_value):
    extent = values.shape
    place = [jax.random.randint(jax.random.fold_in(key, axis), (), 0, extent[axis]) for axis in range(len(extent))]
    values = values.at[tuple(place)].set(least)
    longest = extent.index(max(extent))
    place[longest] = (place[longest] + 1) % extent[longest]
    return values.at[tuple(place)].set(top_value)


def level_of(key, dims, cuts, smallest, top_value):
    gain, own = 1.0, jax.random.fold_in(key, 6)
    for position, parts in cuts:
        draws = jnp.exp(jax.random.uniform(jax.random.fold_in(own, position), (parts,), jnp.float32, smallest / len(cuts), top_value / len(cuts)))
        gain = gain * jnp.repeat(draws, dims[position] // parts).reshape([-1 if axis == position else 1 for axis in range(len(dims))])
    return gain


def noise(own_key, dims, deviation, limit, cuts=(), kind=jnp.bfloat16):
    array = deviation * jax.random.normal(own_key, dims, jnp.float32)
    if cuts:
        array = array * level_of(own_key, dims, cuts, -0.22, 0.18)
    return jnp.clip(array, -limit, limit).astype(kind)


def setup_inputs(seed: int = 0) -> dict:
    arg_keys = jax.random.split(jax.random.key(seed), 5)
    source = noise(arg_keys[0], (NODES, FEATURES), 1.0, 6.0, ((0, 128),), jnp.float32)
    value = draw_value(jax.random.fold_in(arg_keys[4], 71), 0)
    occupancy = plant((jax.random.randint(arg_keys[2], (NODES // BLOCK, NODES // BLOCK), 0, 2) < 1).astype(jnp.int32), jax.random.fold_in(arg_keys[2], 1), 0, 1)
    exponent = draw_exponent(jax.random.fold_in(arg_keys[4], 71), 0)
    return {"source": source, "value": value, "occupancy": occupancy, "exponent": exponent}


EPSILON = 1e-05
RETAIN = 0.8
TELEPORT = 0.2

def block_values(value_rows, occupied_rows, exponent_rows):
    row_count = value_rows.shape[0]
    dense_tile = value_rows.astype(jnp.float32)
    scales = occupied_rows.astype(jnp.float32) * jnp.exp2(exponent_rows.astype(jnp.float32))
    blocked = dense_tile.reshape(row_count // BLOCK, BLOCK, NODES // BLOCK, BLOCK) * scales[:, None, :, None]
    return blocked.reshape(row_count, NODES)

def reference(source, value, occupancy, exponent):
    row_count = NODES // N_ROW

    def propagate(current):
        permuted = current.reshape(N_ROW, N_COL, SPAN, FEATURES).transpose(1, 0, 2, 3).reshape(NODES, FEATURES)

        def row_group(group_index):
            first_row = group_index * row_count
            first_block = group_index * (row_count // BLOCK)
            value_rows = lax.dynamic_slice_in_dim(value, first_row, row_count, 0)
            occupied_rows = lax.dynamic_slice_in_dim(occupancy, first_block, row_count // BLOCK, 0)
            exponent_rows = lax.dynamic_slice_in_dim(exponent, first_block, row_count // BLOCK, 0)
            dense_tile = block_values(value_rows, occupied_rows, exponent_rows)
            energy = lax.optimization_barrier(jnp.sum(dense_tile * dense_tile, axis=1))
            inverse = 1.0 / (jnp.sqrt(NODES * 1.0) * jnp.sqrt(energy / NODES + EPSILON))
            product = jnp.dot(dense_tile, permuted, precision=lax.Precision.HIGHEST, preferred_element_type=jnp.float32)
            return product * inverse[:, None]
        mixing = lax.map(row_group, jnp.arange(N_ROW, dtype=jnp.int32))
        return mixing.reshape(NODES, FEATURES)
    current = source
    for iteration in range(STEPS):
        current = jnp.tanh(RETAIN * propagate(current) + TELEPORT * source)
    return current
```

```python
import jax
import jax.numpy as jnp
from jax import lax
from jax.experimental import pallas as pl
from jax.experimental.pallas import tpu as pltpu
from jax.sharding import PartitionSpec as P

STEPS = 3
EPSILON = 1e-05
RETAIN = 0.8
TELEPORT = 0.2
NODES = 32768
F32, BF16 = jnp.float32, jnp.bfloat16
MESH = pl.DeviceIdType.MESH
VMEM = pltpu.VMEM


def low_lanes(rows=128):
    return lax.broadcasted_iota(jnp.int32, (rows, 128), 1) < 64


def fold(top, bottom):
    low = low_lanes(top.shape[0])
    return jnp.where(low, top, bottom) + pltpu.roll(jnp.where(low, bottom, top), 64, 1)


def kernel(
    src_ref, val_ref, occ_ref, exp_ref, out_ref,
    a_ref, scale_ref, x_ref, rhs_ref, acc_ref, psrc_ref, inv_ref,
    core_out, core_in, col_out, col_in,
    e_part, e_core, e_out, e_in, last_ref,
    load_sem, ag_ss, ag_rs, core_ss, core_rs, col_ss, col_rs,
    ec_ss, ec_rs, e_ss, e_rs,
):
    row, col = lax.axis_index("row"), lax.axis_index("col")
    yh, x = row // 4, row % 4
    z, yl, core = col // 4, (col // 2) % 2, col % 2
    sibling = (row, z * 4 + yl * 2 + 1 - core)

    loads = []
    for c in range(16):
        place = (c % 2) * 8 + c // 2
        loads.append(
            pltpu.make_async_copy(
                val_ref.at[pl.ds(c * 256, 256)],
                a_ref.at[pl.ds(place * 256, 256)],
                load_sem.at[c],
            )
        )
        loads[-1].start()

    row_mates = []
    for dy in (0, 1):
        for dx in (1, 3, 2, 0):
            if dx or dy:
                row_mates.append((((yh + dy) % 2) * 4 + (x + dx) % 4, col))
    col_mates = []
    for dz in (2, 1, 3, 0):
        for dy in (1, 0):
            if dz or dy:
                zz, yy = (z + dz) % 4, (yl + dy) % 2
                col_mates.append((zz * 2 + yy, (row, zz * 4 + yy * 2 + core)))

    barrier = pltpu.get_barrier_semaphore()
    mates = row_mates + [m for _, m in col_mates] + [sibling]
    for mate in mates:
        pl.semaphore_signal(barrier, inc=1, device_id=mate, device_id_type=MESH)

    low = low_lanes()
    top, bottom = src_ref[0:128], src_ref[128:256]
    packed = (
        jnp.where(low, top, pltpu.roll(bottom, 64, 1)),
        jnp.where(low, pltpu.roll(top, 64, 1), bottom),
    )
    for h in range(2):
        psrc_ref[h] = packed[h]
        x_ref[0, h, row] = packed[h]
    pl.semaphore_wait(barrier, len(mates))

    def spread(s, h):
        copies = []
        for i, mate in enumerate(row_mates):
            copies.append(
                pltpu.make_async_remote_copy(
                    x_ref.at[s, h, row], x_ref.at[s, h, row],
                    ag_ss.at[s, h, mate[0]], ag_rs.at[s, h, row],
                    device_id=mate, device_id_type=MESH,
                )
            )
        return copies

    def arrival(s, h, a):
        return pltpu.make_async_remote_copy(
            x_ref.at[s, h, a], x_ref.at[s, h, a],
            ag_ss.at[s, h, a], ag_rs.at[s, h, a],
            device_id=(a, col), device_id_type=MESH,
        )

    def to_sibling(s, h, zz):
        return pltpu.make_async_remote_copy(
            core_out.at[s, h, zz], core_in.at[s, h, zz],
            core_ss.at[s, h, zz], core_rs.at[s, h, zz],
            device_id=sibling, device_id_type=MESH,
        )

    def to_owner(s, h, zz, yy):
        return pltpu.make_async_remote_copy(
            col_out.at[s, h, zz * 2 + yy], col_in.at[s, h, z * 2 + yl],
            col_ss.at[s, h, zz * 2 + yy], col_rs.at[s, h, z * 2 + yl],
            device_id=(row, zz * 4 + yy * 2 + core), device_id_type=MESH,
        )

    def from_mate(s, h, slot, mate):
        return pltpu.make_async_remote_copy(
            col_out.at[s, h, slot], col_in.at[s, h, slot],
            col_ss.at[s, h, slot], col_rs.at[s, h, slot],
            device_id=mate, device_id_type=MESH,
        )

    for h in range(2):
        for copy in spread(0, h):
            copy.start()

    occ = occ_ref[...].astype(F32)
    scale = occ * ((jnp.int32(1) << (exp_ref[...] + 3)).astype(F32) * 0.125)
    for j in range(16):
        scale_ref[:, j * 128 : (j + 1) * 128] = jnp.broadcast_to(scale[:, j : j + 1], (32, 128))
    ones = jnp.ones((8, 128), F32)
    for c in range(16):
        loads[c].wait()
        place = (c % 2) * 8 + c // 2

        for half in range(2):
            def tile(i, _, place=place, half=half, c=c):
                base = pl.multiple_of(place * 256 + half * 128 + i * 16, 16)
                total = jnp.zeros((16, 128), F32)
                for j in range(16):
                    lanes = slice(j * 128, (j + 1) * 128)
                    part = a_ref[pl.ds(base, 16), lanes].astype(F32)
                    part = part * scale_ref[c * 2 + half : c * 2 + half + 1, lanes]
                    total += part * part
                    a_ref[pl.ds(base, 16), lanes] = part.astype(BF16)
                acc_ref[pl.ds(half * 128 + i * 16, 16), :] = total
                return 0

            lax.fori_loop(0, 8, tile, 0, unroll=2)
        e_part[c % 2, c // 2] = lax.dot_general(
            ones, acc_ref[0:256, :], (((1,), (1,)), ((), ())),
            precision=lax.Precision.HIGHEST, preferred_element_type=F32,
        )
    e_sib = pltpu.make_async_remote_copy(
        e_part.at[1 - core], e_core, ec_ss, ec_rs, device_id=sibling, device_id_type=MESH
    )
    e_sib.start()
    e_sib.wait()
    e_out[...] = e_part[core] + e_core[...]
    e_copies = []
    for slot, mate in col_mates:
        copy = pltpu.make_async_remote_copy(
            e_out.at[slot], e_in.at[z * 2 + yl], e_ss.at[slot], e_rs.at[z * 2 + yl],
            device_id=mate, device_id_type=MESH,
        )
        copy.start()
        e_copies.append(copy)

    def load_rhs(s, h, a):
        part = x_ref[s, h, a]
        high = part.astype(BF16).astype(F32)
        rest = pltpu.roll(part - high, 64, 1)
        base = pl.multiple_of(a * 256, 256)
        rhs_ref[pl.ds(base, 128), :] = jnp.where(low, high, rest).astype(BF16)
        rhs_ref[pl.ds(base + 128, 128), :] = jnp.where(low, rest, high).astype(BF16)

    near = pl.multiple_of(yh * 1024, 1024)
    far = pl.multiple_of((1 - yh) * 1024, 1024)

    def multiply(s, h):
        load_rhs(s, h, row)
        for dx in (1, 3, 2):
            a = yh * 4 + (x + dx) % 4
            arrival(s, h, a).wait_recv()
            load_rhs(s, h, a)

        def first(m, _):
            rows = pl.ds(pl.multiple_of(m * 512, 512), 512)
            acc_ref[rows, :] = jnp.dot(
                a_ref[rows, pl.ds(near, 1024)], rhs_ref[pl.ds(near, 1024), :],
                preferred_element_type=F32,
            )
            return 0

        lax.fori_loop(0, 8, first, 0)
        for dx in (1, 3, 2, 0):
            a = (1 - yh) * 4 + (x + dx) % 4
            arrival(s, h, a).wait_recv()
            load_rhs(s, h, a)

        def second(whose, zz):
            rows = pl.ds(pl.multiple_of(whose * 2048 + zz * 512, 512), 512)
            total = acc_ref[rows, :] + jnp.dot(
                a_ref[rows, pl.ds(far, 1024)], rhs_ref[pl.ds(far, 1024), :],
                preferred_element_type=F32,
            )
            return [fold(total[y * 256 : y * 256 + 128], total[y * 256 + 128 : y * 256 + 256]) for y in (0, 1)]

        def theirs(it, _):
            zz = (z + 1 + it) % 4
            blocks = second(1 - core, zz)
            for y in (0, 1):
                core_out[s, h, zz, y] = blocks[y]
            to_sibling(s, h, zz).start()
            return 0

        lax.fori_loop(0, 4, theirs, 0)

        def mine(it, _):
            zz = (z + 1 + it) % 4
            blocks = second(core, zz)
            to_sibling(s, h, zz).wait_recv()
            for y in (0, 1):
                col_out[s, h, zz * 2 + y] = blocks[y] + core_in[s, h, zz, y]

            @pl.when(it != 3)
            def _():
                for dy in (1, 0):
                    to_owner(s, h, zz, (yl + dy) % 2).start()

            @pl.when(it == 3)
            def _():
                to_owner(s, h, z, 1 - yl).start()

            return 0

        lax.fori_loop(0, 4, mine, 0)

    def finish(s, h):
        total = col_out[s, h, z * 2 + yl]
        for slot, mate in col_mates:
            from_mate(s, h, slot, mate).wait_recv()
            total = total + col_in[s, h, slot]
        new = jnp.tanh(RETAIN * total * inv_ref[...] + TELEPORT * psrc_ref[h])
        if s < STEPS - 1:
            x_ref[s + 1, h, row] = new
            for copy in spread(s + 1, h):
                copy.start()
        else:
            last_ref[h] = new

    for s in range(STEPS):
        for h in range(2):
            multiply(s, h)
        if s == 0:
            energy = e_out[z * 2 + yl]
            for slot, mate in col_mates:
                pltpu.make_async_remote_copy(
                    e_out.at[slot], e_in.at[slot], e_ss.at[slot], e_rs.at[slot],
                    device_id=mate, device_id_type=MESH,
                ).wait_recv()
                energy = energy + e_in[slot]
            across = [
                jnp.transpose(jnp.broadcast_to(energy[0:1, k * 128 : (k + 1) * 128], (128, 128)))
                for k in range(2)
            ]
            mean = jnp.where(low, across[0], across[1]) / NODES
            inv_ref[...] = 1.0 / (jnp.sqrt(NODES * 1.0) * jnp.sqrt(mean + EPSILON))
        for h in range(2):
            finish(s, h)

    left, right = last_ref[0], last_ref[1]
    out_ref[0:128] = jnp.where(low, left, pltpu.roll(right, 64, 1))
    out_ref[128:256] = jnp.where(low, pltpu.roll(left, 64, 1), right)

    for copy in e_copies:
        copy.wait_send()
    for s in range(STEPS):
        for h in range(2):
            for copy in spread(s, h):
                copy.wait_send()
            for zz in range(4):
                to_sibling(s, h, zz).wait_send()
            for slot, mate in col_mates:
                from_mate(s, h, slot, mate).wait_send()


def shards(source, value, occupancy, exponent):
    vmem = pl.BlockSpec(memory_space=VMEM)
    dma = pltpu.SemaphoreType.DMA
    halves = (STEPS, 2)
    return pl.pallas_call(
        kernel,
        out_shape=jax.ShapeDtypeStruct((256, 128), F32),
        in_specs=[vmem, pl.BlockSpec(memory_space=pl.ANY), vmem, vmem],
        out_specs=vmem,
        scratch_shapes=[
            VMEM((4096, 2048), BF16),
            VMEM((32, 2048), F32),
            VMEM((*halves, 8, 128, 128), F32),
            VMEM((2048, 128), BF16),
            VMEM((4096, 128), F32),
            VMEM((2, 128, 128), F32),
            VMEM((128, 128), F32),
            VMEM((*halves, 4, 2, 128, 128), F32),
            VMEM((*halves, 4, 2, 128, 128), F32),
            VMEM((*halves, 8, 128, 128), F32),
            VMEM((*halves, 8, 128, 128), F32),
            VMEM((2, 8, 8, 256), F32),
            VMEM((8, 8, 256), F32),
            VMEM((8, 8, 256), F32),
            VMEM((8, 8, 256), F32),
            VMEM((2, 128, 128), F32),
            dma((16,)),
            dma((*halves, 8)), dma((*halves, 8)),
            dma((*halves, 4)), dma((*halves, 4)),
            dma((*halves, 8)), dma((*halves, 8)),
            dma, dma,
            dma((8,)), dma((8,)),
        ],
        compiler_params=pltpu.CompilerParams(
            collective_id=0, has_side_effects=True, vmem_limit_bytes=58 * 2**20
        ),
        cost_estimate=pl.CostEstimate(
            flops=3 * 2 * 4096 * 2048 * 256, bytes_accessed=17 * 2**20, transcendentals=3 * 32768
        ),
    )(source, value, occupancy, exponent)


def solution(mesh):
    placed = (P(("row", "col"), None), P("row", "col"), P("row", "col"), P("row", "col"))
    return jax.shard_map(
        shards, mesh=mesh, in_specs=placed, out_specs=P(("row", "col"), None), check_vma=False
    )
```

```python
import jax
import jax.numpy as jnp
from jax import lax
from jax.experimental import pallas as pl
from jax.experimental.pallas import tpu as pltpu
from jax.sharding import PartitionSpec as P

STEPS = 3
EPSILON = 1e-05
RETAIN = 0.8
TELEPORT = 0.2
NODES = 32768
FORWARDED = (1, 3, 2)
AHEAD = 6
F32, BF16 = jnp.float32, jnp.bfloat16
MESH = pl.DeviceIdType.MESH
VMEM = pltpu.VMEM


def low_lanes(rows=128):
    return lax.broadcasted_iota(jnp.int32, (rows, 128), 1) < 64


def fold(top, bottom):
    low = low_lanes(top.shape[0])
    return jnp.where(low, top, bottom) + pltpu.roll(jnp.where(low, bottom, top), 64, 1)


def kernel(
    src_hbm, val_ref, occ_hbm, exp_hbm, out_ref,
    src_ref, occ_ref, exp_ref, small_sem,
    stage_ref, a_ref, scale_ref, x_ref, rhs_ref, acc_ref, psrc_ref, inv_ref,
    core_out, core_in, col_out, col_in,
    squares, tall, e_part, e_core, e_out, e_in, last_ref,
    load_sem, ag_ss, ag_rs, core_ss, core_rs, col_ss, col_rs,
    ec_ss, ec_rs, e_ss, e_rs,
):
    row, col = lax.axis_index("row"), lax.axis_index("col")
    yh, x = row // 4, row % 4
    z, yl, core = col // 4, (col // 2) % 2, col % 2
    sibling = (row, z * 4 + yl * 2 + 1 - core)

    def load(place):
        owner = place % 8 * 2 + place // 8
        return pltpu.make_async_copy(
            val_ref.at[pl.ds(pl.multiple_of(owner * 256, 256), 256)],
            stage_ref.at[place % AHEAD],
            load_sem.at[place],
        )

    small = [
        pltpu.make_async_copy(there, here, small_sem.at[k])
        for k, (there, here) in enumerate(
            [(src_hbm, src_ref), (occ_hbm, occ_ref), (exp_hbm, exp_ref)]
        )
    ]
    for copy in small:
        copy.start()

    row_mates = []
    for dy in (0, 1):
        for dx in (1, 3, 2, 0):
            if dx or dy:
                row_mates.append((((yh + dy) % 2) * 4 + (x + dx) % 4, col))
    col_mates = []
    for dz in (2, 1, 3, 0):
        for dy in (1, 0):
            if dz or dy:
                zz, yy = (z + dz) % 4, (yl + dy) % 2
                col_mates.append((zz * 2 + yy, (row, zz * 4 + yy * 2 + core)))

    barrier = pltpu.get_barrier_semaphore()
    mates = row_mates + [m for _, m in col_mates] + [sibling]
    for mate in mates:
        pl.semaphore_signal(barrier, inc=1, device_id=mate, device_id_type=MESH)

    for place in range(AHEAD):
        load(place).start()
    low = low_lanes()
    small[0].wait()
    top, bottom = src_ref[0:128], src_ref[128:256]
    packed = (
        jnp.where(low, top, pltpu.roll(bottom, 64, 1)),
        jnp.where(low, pltpu.roll(top, 64, 1), bottom),
    )
    for h in range(2):
        psrc_ref[h] = packed[h]
        x_ref[0, h, row] = packed[h]
    pl.semaphore_wait(barrier, len(mates))

    partner = (1 - yh) * 4 + x

    def spread(s, h):
        mates = [partner] + [yh * 4 + (x + dx) % 4 for dx in (1, 3, 2)]
        mates += [(1 - yh) * 4 + (x + dx) % 4 for dx in (2, 1, 3) if s == 0 or dx not in FORWARDED]
        return [
            pltpu.make_async_remote_copy(
                x_ref.at[s, h, row], x_ref.at[s, h, row],
                ag_ss.at[s, h, mate], ag_rs.at[s, h, row],
                device_id=(mate, col), device_id_type=MESH,
            )
            for mate in mates
        ]

    def forward(s, h):
        if s == 0:
            return []
        return [
            pltpu.make_async_remote_copy(
                x_ref.at[s, h, partner], x_ref.at[s, h, partner],
                ag_ss.at[s, h, 8 + dx], ag_rs.at[s, h, partner],
                device_id=(yh * 4 + (x + dx) % 4, col), device_id_type=MESH,
            )
            for dx in FORWARDED
        ]

    def pass_on(s, h):
        arrival(s, h, partner).wait_recv()
        for copy in forward(s, h):
            copy.start()

    def arrival(s, h, a):
        return pltpu.make_async_remote_copy(
            x_ref.at[s, h, a], x_ref.at[s, h, a],
            ag_ss.at[s, h, a], ag_rs.at[s, h, a],
            device_id=(a, col), device_id_type=MESH,
        )

    def to_sibling(s, h, pair):
        return pltpu.make_async_remote_copy(
            core_out.at[s, h, pair], core_in.at[s, h, pair],
            core_ss.at[s, h, pair], core_rs.at[s, h, pair],
            device_id=sibling, device_id_type=MESH,
        )

    def to_owner(s, h, zz, yy):
        return pltpu.make_async_remote_copy(
            col_out.at[s, h, zz * 2 + yy], col_in.at[s, h, z * 2 + yl],
            col_ss.at[s, h, zz * 2 + yy], col_rs.at[s, h, z * 2 + yl],
            device_id=(row, zz * 4 + yy * 2 + core), device_id_type=MESH,
        )

    def from_mate(s, h, slot, mate):
        return pltpu.make_async_remote_copy(
            col_out.at[s, h, slot], col_in.at[s, h, slot],
            col_ss.at[s, h, slot], col_rs.at[s, h, slot],
            device_id=mate, device_id_type=MESH,
        )

    for copy in spread(0, 0):
        copy.start()

    small[1].wait()
    small[2].wait()
    tall[...] = jnp.zeros_like(tall)
    tall[0:16, 0:32] = occ_ref[...].astype(F32) * (
        (jnp.int32(1) << (exp_ref[...] + 3)).astype(F32) * 0.125
    )
    scale = jnp.transpose(tall[...])
    for j in range(16):
        across = jnp.broadcast_to(scale[0:32, j : j + 1], (32, 128))
        for i in range(32):
            scale_ref[i, :, j * 128 : (j + 1) * 128] = jnp.broadcast_to(
                across[i : i + 1], (16, 128)
            ).astype(BF16)

    squares[0:256, :] = jnp.zeros((256, 128), F32)

    def sum_lanes(place):
        ones = jnp.ones((8, 128), BF16)
        dims = (((1,), (1,)), ((), ()))
        part = squares[pl.ds(pl.multiple_of(place * 256, 256), 256), :]
        high = part.astype(BF16)
        rest = (part - high.astype(F32)).astype(BF16)
        e_part[place // 8, place % 8] = lax.dot_general(
            ones, high, dims, preferred_element_type=F32
        ) + lax.dot_general(ones, rest, dims, preferred_element_type=F32)

    def base_of(a):
        return ((a // 4 + yh) % 2 * 4 + (a % 4 + 4 - x) % 4) * 256

    bases = [base_of(a) for a in range(8)]

    def scale_rows(place, _):
        load(place).wait()
        owner = place % 8 * 2 + place // 8
        slot = place % AHEAD
        sum_lanes(jnp.maximum(place - 1, 0))
        for half in range(2):
            base = pl.multiple_of(place * 256 + half * 128, 128)
            for q in range(4):
                total = [jnp.zeros((16, 128), F32)] * 2
                rows = [pl.ds(half * 128 + q * 32 + r * 16, 16) for r in range(2)]
                out_rows = [pl.ds(base + q * 32 + r * 16, 16) for r in range(2)]
                for j in range(16):
                    lanes = slice(j * 128, (j + 1) * 128)
                    out_lanes = pl.ds(pl.multiple_of(bases[j // 2] + j % 2 * 128, 128), 128)
                    factor = scale_ref[owner * 2 + half, :, lanes]
                    for r in range(2):
                        part = stage_ref[slot, rows[r], lanes] * factor
                        a_ref[out_rows[r], out_lanes] = part
                        wide = part.astype(F32)
                        total[r] = total[r] + wide * wide
                for r in range(2):
                    squares[out_rows[r], :] = total[r]

        @pl.when(place < 16 - AHEAD)
        def _():
            load(place + AHEAD).start()

        return 0

    lax.fori_loop(0, 16, scale_rows, 0)
    sum_lanes(15)
    for copy in spread(0, 1):
        copy.start()

    e_sib = pltpu.make_async_remote_copy(
        e_part.at[1 - core], e_core, ec_ss, ec_rs, device_id=sibling, device_id_type=MESH
    )

    def e_mate(slot, mate, there):
        return pltpu.make_async_remote_copy(
            e_out.at[slot], e_in.at[there], e_ss.at[slot], e_rs.at[there],
            device_id=mate, device_id_type=MESH,
        )

    def send_energy():
        e_sib.wait()
        e_out[...] = e_part[core] + e_core[...]
        for slot, mate in col_mates:
            e_mate(slot, mate, z * 2 + yl).start()

    def take_energy():
        energy = e_out[z * 2 + yl]
        for slot, mate in col_mates:
            e_mate(slot, mate, slot).wait_recv()
            energy = energy + e_in[slot]
        across = [
            jnp.transpose(jnp.broadcast_to(energy[0:1, k * 128 : (k + 1) * 128], (128, 128)))
            for k in range(2)
        ]
        mean = jnp.where(low, across[0], across[1]) / NODES
        inv_ref[...] = 1.0 / (jnp.sqrt(NODES * 1.0) * jnp.sqrt(mean + EPSILON))

    def load_rhs(s, h, a):
        part = x_ref[s, h, a]
        high = part.astype(BF16).astype(F32)
        rest = pltpu.roll(part - high, 64, 1)
        base = pl.multiple_of(base_of(a), 256)
        rhs_ref[pl.ds(base, 128), :] = jnp.where(low, high, rest).astype(BF16)
        rhs_ref[pl.ds(base + 128, 128), :] = jnp.where(low, rest, high).astype(BF16)

    def multiply_near(s, h):
        load_rhs(s, h, row)
        load_rhs(s, h, partner)
        for dx in (1, 3, 2):
            a = yh * 4 + (x + dx) % 4
            arrival(s, h, a).wait_recv()
            load_rhs(s, h, a)

        def tile(m, _):
            rows = pl.ds(pl.multiple_of(m * 1024, 1024), 1024)
            acc_ref[rows, :] = jnp.dot(
                a_ref[rows, 0:1280], rhs_ref[0:1280, :],
                preferred_element_type=F32,
            )
            return 0

        lax.fori_loop(0, 4, tile, 0)

    def far_tile(whose, pair):
        rows = pl.ds(pl.multiple_of(whose * 2048 + pair * 1024, 1024), 1024)
        total = acc_ref[rows, :] + jnp.dot(
            a_ref[rows, 1280:2048], rhs_ref[1280:2048, :],
            preferred_element_type=F32,
        )
        return [fold(total[b * 256 : b * 256 + 128], total[b * 256 + 128 : b * 256 + 256]) for b in range(4)]

    def multiply_far(s, h):
        for dx in (1, 3, 2):
            a = (1 - yh) * 4 + (x + dx) % 4
            arrival(s, h, a).wait_recv()
            load_rhs(s, h, a)

        def theirs(it, _):
            pair = (z // 2 + 1 + it) % 2
            blocks = far_tile(1 - core, pair)
            for b in range(4):
                core_out[s, h, pair, b] = blocks[b]
            to_sibling(s, h, pair).start()
            return 0

        lax.fori_loop(0, 2, theirs, 0)

    def join(s, h):
        def mine(it, _):
            pair = (z // 2 + 1 + it) % 2
            blocks = far_tile(core, pair)
            to_sibling(s, h, pair).wait_recv()
            for b in range(4):
                col_out[s, h, pair * 4 + b] = blocks[b] + core_in[s, h, pair, b]
            for dz in (1, 0):
                zz = pair * 2 + (z + dz) % 2
                for dy in (1, 0):
                    if dz or dy:
                        to_owner(s, h, zz, (yl + dy) % 2).start()
                    else:

                        @pl.when(it == 0)
                        def _():
                            to_owner(s, h, zz, yl).start()

            return 0

        lax.fori_loop(0, 2, mine, 0)

    def finish(s, h):
        total = col_out[s, h, z * 2 + yl]
        for slot, mate in col_mates:
            from_mate(s, h, slot, mate).wait_recv()
            total = total + col_in[s, h, slot]
        new = jnp.tanh(RETAIN * total * inv_ref[...] + TELEPORT * psrc_ref[h])
        if s < STEPS - 1:
            x_ref[s + 1, h, row] = new
            for copy in spread(s + 1, h):
                copy.start()
        else:
            last_ref[h] = new

    pass_on(0, 0)
    e_sib.start()
    multiply_near(0, 0)
    multiply_far(0, 0)
    send_energy()
    join(0, 0)
    for s in range(STEPS):
        pass_on(s, 1)
        multiply_near(s, 1)
        if s == 0:
            take_energy()
        multiply_far(s, 1)
        if s < STEPS - 1:
            finish(s, 0)
            join(s, 1)
            pass_on(s + 1, 0)
            multiply_near(s + 1, 0)
            multiply_far(s + 1, 0)
            finish(s, 1)
            join(s + 1, 0)
        else:
            join(s, 1)
            finish(s, 0)
            finish(s, 1)

    left, right = last_ref[0], last_ref[1]
    out_ref[0:128] = jnp.where(low, left, pltpu.roll(right, 64, 1))
    out_ref[128:256] = jnp.where(low, pltpu.roll(left, 64, 1), right)

    for slot, mate in col_mates:
        e_mate(slot, mate, slot).wait_send()
    for s in range(STEPS):
        for h in range(2):
            for copy in spread(s, h) + forward(s, h):
                copy.wait_send()
            for pair in range(2):
                to_sibling(s, h, pair).wait_send()
            for slot, mate in col_mates:
                from_mate(s, h, slot, mate).wait_send()


def shards(source, value, occupancy, exponent):
    vmem = pl.BlockSpec(memory_space=VMEM)
    dma = pltpu.SemaphoreType.DMA
    halves = (STEPS, 2)
    return pl.pallas_call(
        kernel,
        out_shape=jax.ShapeDtypeStruct((256, 128), F32),
        in_specs=[pl.BlockSpec(memory_space=pltpu.HBM)] * 4,
        out_specs=vmem,
        scratch_shapes=[
            VMEM((256, 128), F32),
            VMEM((16, 32), jnp.int32),
            VMEM((16, 32), jnp.int32),
            dma((3,)),
            VMEM((AHEAD, 256, 2048), BF16),
            VMEM((4096, 2048), BF16),
            VMEM((32, 16, 2048), BF16),
            VMEM((*halves, 8, 128, 128), F32),
            VMEM((2048, 128), BF16),
            VMEM((4096, 128), F32),
            VMEM((2, 128, 128), F32),
            VMEM((128, 128), F32),
            VMEM((*halves, 2, 4, 128, 128), F32),
            VMEM((*halves, 2, 4, 128, 128), F32),
            VMEM((*halves, 8, 128, 128), F32),
            VMEM((*halves, 8, 128, 128), F32),
            VMEM((4096, 128), F32),
            VMEM((128, 128), F32),
            VMEM((2, 8, 8, 256), F32),
            VMEM((8, 8, 256), F32),
            VMEM((8, 8, 256), F32),
            VMEM((8, 8, 256), F32),
            VMEM((2, 128, 128), F32),
            dma((16,)),
            dma((*halves, 12)), dma((*halves, 8)),
            dma((*halves, 2)), dma((*halves, 2)),
            dma((*halves, 8)), dma((*halves, 8)),
            dma, dma,
            dma((8,)), dma((8,)),
        ],
        compiler_params=pltpu.CompilerParams(
            collective_id=0, has_side_effects=True, vmem_limit_bytes=58 * 2**20
        ),
        cost_estimate=pl.CostEstimate(
            flops=3 * 2 * 4096 * 2048 * 256, bytes_accessed=17 * 2**20, transcendentals=3 * 32768
        ),
    )(source, value, occupancy.T, exponent.T)


def solution(mesh):
    placed = (P(("row", "col"), None), P("row", "col"), P("row", "col"), P("row", "col"))
    return jax.shard_map(
        shards, mesh=mesh, in_specs=placed, out_specs=P(("row", "col"), None), check_vma=False
    )
```

```python
import jax
import jax.numpy as jnp
from jax import lax
from jax.experimental import pallas as pl
from jax.experimental.pallas import tpu as pltpu
from jax.sharding import PartitionSpec as P

STEPS = 3
EPSILON = 1e-05
RETAIN = 0.8
TELEPORT = 0.2
NODES = 32768
FORWARDED = (1, 3, 2)
AHEAD = 6
CHUNKS = 2
CHUNK = 128 // CHUNKS
F32, BF16 = jnp.float32, jnp.bfloat16
MESH = pl.DeviceIdType.MESH
VMEM = pltpu.VMEM


def low_lanes(rows=128):
    return lax.broadcasted_iota(jnp.int32, (rows, 128), 1) < 64


def fold(top, bottom):
    low = low_lanes(top.shape[0])
    return jnp.where(low, top, bottom) + pltpu.roll(jnp.where(low, bottom, top), 64, 1)


def kernel(
    src_hbm, val_ref, occ_hbm, exp_hbm, out_ref,
    src_ref, occ_ref, exp_ref, small_sem,
    stage_ref, a_ref, scale_ref, x_ref, rhs_ref, acc_ref, psrc_ref, inv_ref,
    core_out, core_in, col_out, col_in,
    squares, tall, e_part, e_core, e_out, e_in, last_ref,
    load_sem, ag_ss, ag_rs, core_ss, core_rs, col_ss, col_rs,
    ec_ss, ec_rs, e_ss, e_rs,
):
    row, col = lax.axis_index("row"), lax.axis_index("col")
    yh, x = row // 4, row % 4
    z, yl, core = col // 4, (col // 2) % 2, col % 2
    sibling = (row, z * 4 + yl * 2 + 1 - core)

    def load(place):
        owner = place % 8 * 2 + place // 8
        return pltpu.make_async_copy(
            val_ref.at[pl.ds(pl.multiple_of(owner * 256, 256), 256)],
            stage_ref.at[place % AHEAD],
            load_sem.at[place],
        )

    small = [
        pltpu.make_async_copy(there, here, small_sem.at[k])
        for k, (there, here) in enumerate(
            [(src_hbm, src_ref), (occ_hbm, occ_ref), (exp_hbm, exp_ref)]
        )
    ]
    for copy in small:
        copy.start()

    row_mates = []
    for dy in (0, 1):
        for dx in (1, 3, 2, 0):
            if dx or dy:
                row_mates.append((((yh + dy) % 2) * 4 + (x + dx) % 4, col))
    col_mates = []
    for dz in (2, 1, 3, 0):
        for dy in (1, 0):
            if dz or dy:
                zz, yy = (z + dz) % 4, (yl + dy) % 2
                col_mates.append((zz * 2 + yy, (row, zz * 4 + yy * 2 + core)))

    barrier = pltpu.get_barrier_semaphore()
    mates = row_mates + [m for _, m in col_mates] + [sibling]
    for mate in mates:
        pl.semaphore_signal(barrier, inc=1, device_id=mate, device_id_type=MESH)

    for place in range(AHEAD):
        load(place).start()
    low = low_lanes()
    small[0].wait()
    top, bottom = src_ref[0:128], src_ref[128:256]
    packed = (
        jnp.where(low, top, pltpu.roll(bottom, 64, 1)),
        jnp.where(low, pltpu.roll(top, 64, 1), bottom),
    )
    for h in range(2):
        psrc_ref[h] = packed[h]
        x_ref[0, h, row] = packed[h]
    pl.semaphore_wait(barrier, len(mates))

    partner = (1 - yh) * 4 + x

    def rows_of(k):
        return pl.ds(k * CHUNK, CHUNK)

    def gather_copy(s, h, a, k, send, mate):
        return pltpu.make_async_remote_copy(
            x_ref.at[s, h, a, rows_of(k)], x_ref.at[s, h, a, rows_of(k)],
            ag_ss.at[s, h, send, k], ag_rs.at[s, h, a, k],
            device_id=(mate, col), device_id_type=MESH,
        )

    def spread(s, h, k):
        mates = [partner] + [yh * 4 + (x + dx) % 4 for dx in (1, 3, 2)]
        mates += [(1 - yh) * 4 + (x + dx) % 4 for dx in (2, 1, 3) if s == 0 or dx not in FORWARDED]
        return [gather_copy(s, h, row, k, mate, mate) for mate in mates]

    def forward(s, h, k):
        if s == 0:
            return []
        return [
            gather_copy(s, h, partner, k, 8 + dx, yh * 4 + (x + dx) % 4) for dx in FORWARDED
        ]

    def arrive(s, h, a):
        for k in range(CHUNKS):
            gather_copy(s, h, a, k, a, a).wait_recv()

    def pass_on(s, h):
        for k in range(CHUNKS):
            gather_copy(s, h, partner, k, partner, partner).wait_recv()
            for copy in forward(s, h, k):
                copy.start()

    def to_sibling(s, h, pair):
        return pltpu.make_async_remote_copy(
            core_out.at[s, h, pair], core_in.at[s, h, pair],
            core_ss.at[s, h, pair], core_rs.at[s, h, pair],
            device_id=sibling, device_id_type=MESH,
        )

    def to_owner(s, h, zz, yy, k):
        return pltpu.make_async_remote_copy(
            col_out.at[s, h, zz * 2 + yy, rows_of(k)], col_in.at[s, h, z * 2 + yl, rows_of(k)],
            col_ss.at[s, h, zz * 2 + yy, k], col_rs.at[s, h, z * 2 + yl, k],
            device_id=(row, zz * 4 + yy * 2 + core), device_id_type=MESH,
        )

    def from_mate(s, h, slot, mate, k):
        return pltpu.make_async_remote_copy(
            col_out.at[s, h, slot, rows_of(k)], col_in.at[s, h, slot, rows_of(k)],
            col_ss.at[s, h, slot, k], col_rs.at[s, h, slot, k],
            device_id=mate, device_id_type=MESH,
        )

    for k in range(CHUNKS):
        for copy in spread(0, 0, k):
            copy.start()

    small[1].wait()
    small[2].wait()
    tall[...] = jnp.zeros_like(tall)
    tall[0:16, 0:32] = occ_ref[...].astype(F32) * (
        (jnp.int32(1) << (exp_ref[...] + 3)).astype(F32) * 0.125
    )
    scale = jnp.transpose(tall[...])
    for j in range(16):
        across = jnp.broadcast_to(scale[0:32, j : j + 1], (32, 128))
        for i in range(32):
            scale_ref[i, :, j * 128 : (j + 1) * 128] = jnp.broadcast_to(
                across[i : i + 1], (16, 128)
            ).astype(BF16)

    squares[0:256, :] = jnp.zeros((256, 128), F32)

    def sum_lanes(place):
        ones = jnp.ones((8, 128), BF16)
        dims = (((1,), (1,)), ((), ()))
        part = squares[pl.ds(pl.multiple_of(place * 256, 256), 256), :]
        high = part.astype(BF16)
        rest = (part - high.astype(F32)).astype(BF16)
        e_part[place // 8, place % 8] = lax.dot_general(
            ones, high, dims, preferred_element_type=F32
        ) + lax.dot_general(ones, rest, dims, preferred_element_type=F32)

    def base_of(a):
        return ((a // 4 + yh) % 2 * 4 + (a % 4 + 4 - x) % 4) * 256

    bases = [base_of(a) for a in range(8)]

    def scale_rows(place, _):
        load(place).wait()
        owner = place % 8 * 2 + place // 8
        slot = place % AHEAD
        sum_lanes(jnp.maximum(place - 1, 0))
        for half in range(2):
            base = pl.multiple_of(place * 256 + half * 128, 128)
            for q in range(4):
                total = [jnp.zeros((16, 128), F32)] * 2
                rows = [pl.ds(half * 128 + q * 32 + r * 16, 16) for r in range(2)]
                out_rows = [pl.ds(base + q * 32 + r * 16, 16) for r in range(2)]
                for j in range(16):
                    lanes = slice(j * 128, (j + 1) * 128)
                    out_lanes = pl.ds(pl.multiple_of(bases[j // 2] + j % 2 * 128, 128), 128)
                    factor = scale_ref[owner * 2 + half, :, lanes]
                    for r in range(2):
                        part = stage_ref[slot, rows[r], lanes] * factor
                        a_ref[out_rows[r], out_lanes] = part
                        wide = part.astype(F32)
                        total[r] = total[r] + wide * wide
                for r in range(2):
                    squares[out_rows[r], :] = total[r]

        @pl.when(place < 16 - AHEAD)
        def _():
            load(place + AHEAD).start()

        return 0

    lax.fori_loop(0, 16, scale_rows, 0)
    sum_lanes(15)
    for k in range(CHUNKS):
        for copy in spread(0, 1, k):
            copy.start()

    e_sib = pltpu.make_async_remote_copy(
        e_part.at[1 - core], e_core, ec_ss, ec_rs, device_id=sibling, device_id_type=MESH
    )

    def e_mate(slot, mate, there):
        return pltpu.make_async_remote_copy(
            e_out.at[slot], e_in.at[there], e_ss.at[slot], e_rs.at[there],
            device_id=mate, device_id_type=MESH,
        )

    def send_energy():
        e_sib.wait()
        e_out[...] = e_part[core] + e_core[...]
        for slot, mate in col_mates:
            e_mate(slot, mate, z * 2 + yl).start()

    def take_energy():
        energy = e_out[z * 2 + yl]
        for slot, mate in col_mates:
            e_mate(slot, mate, slot).wait_recv()
            energy = energy + e_in[slot]
        across = [
            jnp.transpose(jnp.broadcast_to(energy[0:1, k * 128 : (k + 1) * 128], (128, 128)))
            for k in range(2)
        ]
        mean = jnp.where(low, across[0], across[1]) / NODES
        inv_ref[...] = 1.0 / (jnp.sqrt(NODES * 1.0) * jnp.sqrt(mean + EPSILON))

    def load_rhs(s, h, a):
        part = x_ref[s, h, a]
        high = part.astype(BF16).astype(F32)
        rest = pltpu.roll(part - high, 64, 1)
        base = pl.multiple_of(base_of(a), 256)
        rhs_ref[pl.ds(base, 128), :] = jnp.where(low, high, rest).astype(BF16)
        rhs_ref[pl.ds(base + 128, 128), :] = jnp.where(low, rest, high).astype(BF16)

    def multiply_near(s, h):
        load_rhs(s, h, row)
        load_rhs(s, h, partner)
        for dx in (1, 3, 2):
            a = yh * 4 + (x + dx) % 4
            arrive(s, h, a)
            load_rhs(s, h, a)

        def tile(m, _):
            rows = pl.ds(pl.multiple_of(m * 1024, 1024), 1024)
            acc_ref[rows, :] = jnp.dot(
                a_ref[rows, 0:1280], rhs_ref[0:1280, :],
                preferred_element_type=F32,
            )
            return 0

        lax.fori_loop(0, 4, tile, 0)

    def far_tile(whose, pair):
        rows = pl.ds(pl.multiple_of(whose * 2048 + pair * 1024, 1024), 1024)
        total = acc_ref[rows, :] + jnp.dot(
            a_ref[rows, 1280:2048], rhs_ref[1280:2048, :],
            preferred_element_type=F32,
        )
        return [fold(total[b * 256 : b * 256 + 128], total[b * 256 + 128 : b * 256 + 256]) for b in range(4)]

    def multiply_far(s, h):
        for dx in (1, 3, 2):
            a = (1 - yh) * 4 + (x + dx) % 4
            arrive(s, h, a)
            load_rhs(s, h, a)

        def theirs(it, _):
            pair = (z // 2 + 1 + it) % 2
            blocks = far_tile(1 - core, pair)
            for b in range(4):
                core_out[s, h, pair, b] = blocks[b]
            to_sibling(s, h, pair).start()
            return 0

        lax.fori_loop(0, 2, theirs, 0)

    def join(s, h):
        def mine(it, _):
            pair = (z // 2 + 1 + it) % 2
            blocks = far_tile(core, pair)
            to_sibling(s, h, pair).wait_recv()
            for b in range(4):
                col_out[s, h, pair * 4 + b] = blocks[b] + core_in[s, h, pair, b]

            @pl.when(it == 0)
            def _():
                for b in range(4):
                    to_owner(s, h, pair * 2 + b // 2, b % 2, 0).start()

            return 0

        lax.fori_loop(0, 2, mine, 0)
        last = [(z // 2 * 2 + (z + 1) % 2, 1 - yl), (z // 2 * 2 + (z + 1) % 2, yl), (z, 1 - yl)]
        first = [((z // 2 * 2 + 2 + b // 2) % 4, b % 2) for b in range(4)]
        for zz, yy in last:
            to_owner(s, h, zz, yy, 0).start()
        for k in range(1, CHUNKS):
            for zz, yy in first + last:
                to_owner(s, h, zz, yy, k).start()

    def finish(s, h, k):
        rows = rows_of(k)
        total = col_out[s, h, z * 2 + yl, rows]
        for slot, mate in col_mates:
            from_mate(s, h, slot, mate, k).wait_recv()
            total = total + col_in[s, h, slot, rows]
        new = jnp.tanh(RETAIN * total * inv_ref[rows] + TELEPORT * psrc_ref[h, rows])
        if s < STEPS - 1:
            x_ref[s + 1, h, row, rows] = new
            for copy in spread(s + 1, h, k):
                copy.start()
        else:
            last_ref[h, rows] = new

    pass_on(0, 0)
    e_sib.start()
    multiply_near(0, 0)
    multiply_far(0, 0)
    send_energy()
    join(0, 0)
    for s in range(STEPS):
        pass_on(s, 1)
        multiply_near(s, 1)
        if s == 0:
            take_energy()
        if s < STEPS - 1:
            finish(s, 0, 0)
            multiply_far(s, 1)
            finish(s, 0, 1)
            join(s, 1)
            pass_on(s + 1, 0)
            multiply_near(s + 1, 0)
            finish(s, 1, 0)
            multiply_far(s + 1, 0)
            finish(s, 1, 1)
            join(s + 1, 0)
        else:
            multiply_far(s, 1)
            join(s, 1)
            for h in range(2):
                for k in range(CHUNKS):
                    finish(s, h, k)

    left, right = last_ref[0], last_ref[1]
    out_ref[0:128] = jnp.where(low, left, pltpu.roll(right, 64, 1))
    out_ref[128:256] = jnp.where(low, pltpu.roll(left, 64, 1), right)

    for slot, mate in col_mates:
        e_mate(slot, mate, slot).wait_send()
    for s in range(STEPS):
        for h in range(2):
            for k in range(CHUNKS):
                for copy in spread(s, h, k) + forward(s, h, k):
                    copy.wait_send()
            for pair in range(2):
                to_sibling(s, h, pair).wait_send()
            for slot, mate in col_mates:
                for k in range(CHUNKS):
                    from_mate(s, h, slot, mate, k).wait_send()


def shards(source, value, occupancy, exponent):
    vmem = pl.BlockSpec(memory_space=VMEM)
    dma = pltpu.SemaphoreType.DMA
    halves = (STEPS, 2)
    return pl.pallas_call(
        kernel,
        out_shape=jax.ShapeDtypeStruct((256, 128), F32),
        in_specs=[pl.BlockSpec(memory_space=pltpu.HBM)] * 4,
        out_specs=vmem,
        scratch_shapes=[
            VMEM((256, 128), F32),
            VMEM((16, 32), jnp.int32),
            VMEM((16, 32), jnp.int32),
            dma((3,)),
            VMEM((AHEAD, 256, 2048), BF16),
            VMEM((4096, 2048), BF16),
            VMEM((32, 16, 2048), BF16),
            VMEM((*halves, 8, 128, 128), F32),
            VMEM((2048, 128), BF16),
            VMEM((4096, 128), F32),
            VMEM((2, 128, 128), F32),
            VMEM((128, 128), F32),
            VMEM((*halves, 2, 4, 128, 128), F32),
            VMEM((*halves, 2, 4, 128, 128), F32),
            VMEM((*halves, 8, 128, 128), F32),
            VMEM((*halves, 8, 128, 128), F32),
            VMEM((4096, 128), F32),
            VMEM((128, 128), F32),
            VMEM((2, 8, 8, 256), F32),
            VMEM((8, 8, 256), F32),
            VMEM((8, 8, 256), F32),
            VMEM((8, 8, 256), F32),
            VMEM((2, 128, 128), F32),
            dma((16,)),
            dma((*halves, 12, CHUNKS)), dma((*halves, 8, CHUNKS)),
            dma((*halves, 2)), dma((*halves, 2)),
            dma((*halves, 8, CHUNKS)), dma((*halves, 8, CHUNKS)),
            dma, dma,
            dma((8,)), dma((8,)),
        ],
        compiler_params=pltpu.CompilerParams(
            collective_id=0, has_side_effects=True, vmem_limit_bytes=58 * 2**20
        ),
        cost_estimate=pl.CostEstimate(
            flops=3 * 2 * 4096 * 2048 * 256, bytes_accessed=17 * 2**20, transcendentals=3 * 32768
        ),
    )(source, value, occupancy.T, exponent.T)


def solution(mesh):
    placed = (P(("row", "col"), None), P("row", "col"), P("row", "col"), P("row", "col"))
    return jax.shard_map(
        shards, mesh=mesh, in_specs=placed, out_specs=P(("row", "col"), None), check_vma=False
    )
```

```python
import jax
import jax.numpy as jnp
from jax import lax
from jax.experimental import pallas as pl
from jax.experimental.pallas import tpu as pltpu
from jax.sharding import PartitionSpec as P

STEPS = 3
EPSILON = 1e-05
RETAIN = 0.8
TELEPORT = 0.2
NODES = 32768
FORWARDED = (1, 3, 2)
AHEAD = 6
CHUNKS = 2
CHUNK = 128 // CHUNKS
F32, BF16 = jnp.float32, jnp.bfloat16
MESH = pl.DeviceIdType.MESH
VMEM = pltpu.VMEM


def low_lanes(rows=128):
    return lax.broadcasted_iota(jnp.int32, (rows, 128), 1) < 64


def fold(top, bottom):
    low = low_lanes(top.shape[0])
    return jnp.where(low, top, bottom) + pltpu.roll(jnp.where(low, bottom, top), 64, 1)


def kernel(
    src_hbm, val_ref, occ_hbm, exp_hbm, out_ref,
    src_ref, occ_ref, exp_ref, small_sem,
    stage_ref, a_ref, scale_ref, x_ref, rhs_ref, acc_ref, psrc_ref, inv_ref,
    core_out, core_in, col_out, col_in,
    squares, tall, e_part, e_core, e_out, e_in, last_ref,
    load_sem, ag_ss, ag_rs, core_ss, core_rs, col_ss, col_rs,
    ec_ss, ec_rs, e_ss, e_rs,
):
    row, col = lax.axis_index("row"), lax.axis_index("col")
    yh, x = row // 4, row % 4
    z, yl, core = col // 4, (col // 2) % 2, col % 2
    sibling = (row, z * 4 + yl * 2 + 1 - core)

    def load(place):
        owner = place % 8 * 2 + place // 8
        return pltpu.make_async_copy(
            val_ref.at[pl.ds(pl.multiple_of(owner * 256, 256), 256)],
            stage_ref.at[place % AHEAD],
            load_sem.at[place],
        )

    small = [
        pltpu.make_async_copy(there, here, small_sem.at[k])
        for k, (there, here) in enumerate(
            [(src_hbm, src_ref), (occ_hbm, occ_ref), (exp_hbm, exp_ref)]
        )
    ]
    for copy in small:
        copy.start()

    row_mates = []
    for dy in (0, 1):
        for dx in (1, 3, 2, 0):
            if dx or dy:
                row_mates.append((((yh + dy) % 2) * 4 + (x + dx) % 4, col))
    col_mates = []
    for dz in (2, 1, 3, 0):
        for dy in (1, 0):
            if dz or dy:
                zz, yy = (z + dz) % 4, (yl + dy) % 2
                col_mates.append((zz * 2 + yy, (row, zz * 4 + yy * 2 + core)))

    barrier = pltpu.get_barrier_semaphore()
    mates = row_mates + [m for _, m in col_mates] + [sibling]
    for mate in mates:
        pl.semaphore_signal(barrier, inc=1, device_id=mate, device_id_type=MESH)

    for place in range(AHEAD):
        load(place).start()
    low = low_lanes()
    small[0].wait()
    top, bottom = src_ref[0:128], src_ref[128:256]
    packed = (
        jnp.where(low, top, pltpu.roll(bottom, 64, 1)),
        jnp.where(low, pltpu.roll(top, 64, 1), bottom),
    )
    for h in range(2):
        psrc_ref[h] = packed[h]
        x_ref[0, h, row] = packed[h]
    pl.semaphore_wait(barrier, len(mates))

    partner = (1 - yh) * 4 + x

    def rows_of(k):
        return pl.ds(k * CHUNK, CHUNK)

    def gather_copy(s, h, a, k, send, mate):
        return pltpu.make_async_remote_copy(
            x_ref.at[s, h, a, rows_of(k)], x_ref.at[s, h, a, rows_of(k)],
            ag_ss.at[s, h, send, k], ag_rs.at[s, h, a, k],
            device_id=(mate, col), device_id_type=MESH,
        )

    def spread(s, h, k):
        mates = [partner] + [yh * 4 + (x + dx) % 4 for dx in (1, 3, 2)]
        mates += [(1 - yh) * 4 + (x + dx) % 4 for dx in (2, 1, 3) if (s, h) == (0, 0) or dx not in FORWARDED]
        return [gather_copy(s, h, row, k, mate, mate) for mate in mates]

    def forward(s, h, k):
        if (s, h) == (0, 0):
            return []
        return [
            gather_copy(s, h, partner, k, 8 + dx, yh * 4 + (x + dx) % 4) for dx in FORWARDED
        ]

    def arrive(s, h, a):
        for k in range(CHUNKS):
            gather_copy(s, h, a, k, a, a).wait_recv()

    def pass_on(s, h):
        for k in range(CHUNKS):
            gather_copy(s, h, partner, k, partner, partner).wait_recv()
            for copy in forward(s, h, k):
                copy.start()

    def to_sibling(s, h, pair):
        return pltpu.make_async_remote_copy(
            core_out.at[s, h, pair], core_in.at[s, h, pair],
            core_ss.at[s, h, pair], core_rs.at[s, h, pair],
            device_id=sibling, device_id_type=MESH,
        )

    def to_owner(s, h, zz, yy, k):
        return pltpu.make_async_remote_copy(
            col_out.at[s, h, zz * 2 + yy, rows_of(k)], col_in.at[s, h, z * 2 + yl, rows_of(k)],
            col_ss.at[s, h, zz * 2 + yy, k], col_rs.at[s, h, z * 2 + yl, k],
            device_id=(row, zz * 4 + yy * 2 + core), device_id_type=MESH,
        )

    def from_mate(s, h, slot, mate, k):
        return pltpu.make_async_remote_copy(
            col_out.at[s, h, slot, rows_of(k)], col_in.at[s, h, slot, rows_of(k)],
            col_ss.at[s, h, slot, k], col_rs.at[s, h, slot, k],
            device_id=mate, device_id_type=MESH,
        )

    for k in range(CHUNKS):
        for copy in spread(0, 0, k):
            copy.start()

    small[1].wait()
    small[2].wait()
    tall[...] = jnp.zeros_like(tall)
    tall[0:16, 0:32] = occ_ref[...].astype(F32) * (
        (jnp.int32(1) << (exp_ref[...] + 3)).astype(F32) * 0.125
    )
    scale = jnp.transpose(tall[...])
    for j in range(16):
        across = jnp.broadcast_to(scale[0:32, j : j + 1], (32, 128))
        for i in range(32):
            scale_ref[i, :, j * 128 : (j + 1) * 128] = jnp.broadcast_to(
                across[i : i + 1], (16, 128)
            ).astype(BF16)

    squares[0:256, :] = jnp.zeros((256, 128), F32)

    def sum_lanes(place):
        ones = jnp.ones((8, 128), BF16)
        dims = (((1,), (1,)), ((), ()))
        part = squares[pl.ds(pl.multiple_of(place * 256, 256), 256), :]
        high = part.astype(BF16)
        rest = (part - high.astype(F32)).astype(BF16)
        e_part[place // 8, place % 8] = lax.dot_general(
            ones, high, dims, preferred_element_type=F32
        ) + lax.dot_general(ones, rest, dims, preferred_element_type=F32)

    def base_of(a):
        return ((a // 4 + yh) % 2 * 4 + (a % 4 + 4 - x) % 4) * 256

    bases = [base_of(a) for a in range(8)]

    def scale_rows(place, _):
        load(place).wait()
        owner = place % 8 * 2 + place // 8
        slot = place % AHEAD
        sum_lanes(jnp.maximum(place - 1, 0))
        for half in range(2):
            base = pl.multiple_of(place * 256 + half * 128, 128)
            for q in range(4):
                total = [jnp.zeros((16, 128), F32)] * 2
                rows = [pl.ds(half * 128 + q * 32 + r * 16, 16) for r in range(2)]
                out_rows = [pl.ds(base + q * 32 + r * 16, 16) for r in range(2)]
                for j in range(16):
                    lanes = slice(j * 128, (j + 1) * 128)
                    out_lanes = pl.ds(pl.multiple_of(bases[j // 2] + j % 2 * 128, 128), 128)
                    factor = scale_ref[owner * 2 + half, :, lanes]
                    for r in range(2):
                        part = stage_ref[slot, rows[r], lanes] * factor
                        a_ref[out_rows[r], out_lanes] = part
                        wide = part.astype(F32)
                        total[r] = total[r] + wide * wide
                for r in range(2):
                    squares[out_rows[r], :] = total[r]

        @pl.when(place < 16 - AHEAD)
        def _():
            load(place + AHEAD).start()

        return 0

    lax.fori_loop(0, 16, scale_rows, 0)
    sum_lanes(15)
    for k in range(CHUNKS):
        for copy in spread(0, 1, k):
            copy.start()

    e_sib = pltpu.make_async_remote_copy(
        e_part.at[1 - core], e_core, ec_ss, ec_rs, device_id=sibling, device_id_type=MESH
    )

    def e_mate(slot, mate, there):
        return pltpu.make_async_remote_copy(
            e_out.at[slot], e_in.at[there], e_ss.at[slot], e_rs.at[there],
            device_id=mate, device_id_type=MESH,
        )

    def send_energy():
        e_sib.wait()
        e_out[...] = e_part[core] + e_core[...]
        for slot, mate in col_mates:
            e_mate(slot, mate, z * 2 + yl).start()

    def take_energy():
        energy = e_out[z * 2 + yl]
        for slot, mate in col_mates:
            e_mate(slot, mate, slot).wait_recv()
            energy = energy + e_in[slot]
        across = [
            jnp.transpose(jnp.broadcast_to(energy[0:1, k * 128 : (k + 1) * 128], (128, 128)))
            for k in range(2)
        ]
        mean = jnp.where(low, across[0], across[1]) / NODES
        inv_ref[...] = 1.0 / (jnp.sqrt(NODES * 1.0) * jnp.sqrt(mean + EPSILON))

    def load_rhs(s, h, a):
        part = x_ref[s, h, a]
        high = part.astype(BF16).astype(F32)
        rest = pltpu.roll(part - high, 64, 1)
        base = pl.multiple_of(base_of(a), 256)
        rhs_ref[pl.ds(base, 128), :] = jnp.where(low, high, rest).astype(BF16)
        rhs_ref[pl.ds(base + 128, 128), :] = jnp.where(low, rest, high).astype(BF16)

    def multiply_near(s, h):
        load_rhs(s, h, row)
        load_rhs(s, h, partner)
        for dx in (1, 3, 2):
            a = yh * 4 + (x + dx) % 4
            arrive(s, h, a)
            load_rhs(s, h, a)

        def tile(m, _):
            rows = pl.ds(pl.multiple_of(m * 2048, 2048), 2048)
            acc_ref[rows, :] = jnp.dot(
                a_ref[rows, 0:1280], rhs_ref[0:1280, :],
                preferred_element_type=F32,
            )
            return 0

        lax.fori_loop(0, 2, tile, 0)

    def far_tile(whose, pair):
        rows = pl.ds(pl.multiple_of(whose * 2048 + pair * 1024, 1024), 1024)
        total = acc_ref[rows, :] + jnp.dot(
            a_ref[rows, 1280:2048], rhs_ref[1280:2048, :],
            preferred_element_type=F32,
        )
        return [fold(total[b * 256 : b * 256 + 128], total[b * 256 + 128 : b * 256 + 256]) for b in range(4)]

    def multiply_far(s, h):
        for dx in (1, 3, 2):
            a = (1 - yh) * 4 + (x + dx) % 4
            arrive(s, h, a)
            load_rhs(s, h, a)

        def theirs(it, _):
            pair = (z // 2 + 1 + it) % 2
            blocks = far_tile(1 - core, pair)
            for b in range(4):
                core_out[s, h, pair, b] = blocks[b]
            to_sibling(s, h, pair).start()
            return 0

        lax.fori_loop(0, 2, theirs, 0)

    def join(s, h):
        def mine(it, _):
            pair = (z // 2 + 1 + it) % 2
            blocks = far_tile(core, pair)
            to_sibling(s, h, pair).wait_recv()
            for b in range(4):
                col_out[s, h, pair * 4 + b] = blocks[b] + core_in[s, h, pair, b]

            @pl.when(it == 0)
            def _():
                for b in range(4):
                    to_owner(s, h, pair * 2 + b // 2, b % 2, 0).start()

            return 0

        lax.fori_loop(0, 2, mine, 0)
        last = [(z // 2 * 2 + (z + 1) % 2, 1 - yl), (z // 2 * 2 + (z + 1) % 2, yl), (z, 1 - yl)]
        first = [((z // 2 * 2 + 2 + b // 2) % 4, b % 2) for b in range(4)]
        for zz, yy in last:
            to_owner(s, h, zz, yy, 0).start()
        for k in range(1, CHUNKS):
            for zz, yy in first + last:
                to_owner(s, h, zz, yy, k).start()

    def finish(s, h, k):
        rows = rows_of(k)
        total = col_out[s, h, z * 2 + yl, rows]
        for slot, mate in col_mates:
            from_mate(s, h, slot, mate, k).wait_recv()
            total = total + col_in[s, h, slot, rows]
        new = jnp.tanh(RETAIN * total * inv_ref[rows] + TELEPORT * psrc_ref[h, rows])
        if s < STEPS - 1:
            x_ref[s + 1, h, row, rows] = new
            for copy in spread(s + 1, h, k):
                copy.start()
        else:
            last_ref[h, rows] = new

    pass_on(0, 0)
    e_sib.start()
    multiply_near(0, 0)
    multiply_far(0, 0)
    send_energy()
    join(0, 0)
    for s in range(STEPS):
        pass_on(s, 1)
        multiply_near(s, 1)
        if s == 0:
            take_energy()
        if s < STEPS - 1:
            finish(s, 0, 0)
            multiply_far(s, 1)
            finish(s, 0, 1)
            join(s, 1)
            pass_on(s + 1, 0)
            multiply_near(s + 1, 0)
            finish(s, 1, 0)
            multiply_far(s + 1, 0)
            finish(s, 1, 1)
            join(s + 1, 0)
        else:
            multiply_far(s, 1)
            join(s, 1)
            for h in range(2):
                for k in range(CHUNKS):
                    finish(s, h, k)

    left, right = last_ref[0], last_ref[1]
    out_ref[0:128] = jnp.where(low, left, pltpu.roll(right, 64, 1))
    out_ref[128:256] = jnp.where(low, pltpu.roll(left, 64, 1), right)

    for slot, mate in col_mates:
        e_mate(slot, mate, slot).wait_send()
    for s in range(STEPS):
        for h in range(2):
            for k in range(CHUNKS):
                for copy in spread(s, h, k) + forward(s, h, k):
                    copy.wait_send()
            for pair in range(2):
                to_sibling(s, h, pair).wait_send()
            for slot, mate in col_mates:
                for k in range(CHUNKS):
                    from_mate(s, h, slot, mate, k).wait_send()


def shards(source, value, occupancy, exponent):
    vmem = pl.BlockSpec(memory_space=VMEM)
    dma = pltpu.SemaphoreType.DMA
    halves = (STEPS, 2)
    return pl.pallas_call(
        kernel,
        out_shape=pltpu.VMEM((256, 128), F32),
        in_specs=[pl.BlockSpec(memory_space=pltpu.HBM)] * 4,
        out_specs=vmem,
        scratch_shapes=[
            VMEM((256, 128), F32),
            VMEM((16, 32), jnp.int32),
            VMEM((16, 32), jnp.int32),
            dma((3,)),
            VMEM((AHEAD, 256, 2048), BF16),
            VMEM((4096, 2048), BF16),
            VMEM((32, 16, 2048), BF16),
            VMEM((*halves, 8, 128, 128), F32),
            VMEM((2048, 128), BF16),
            VMEM((4096, 128), F32),
            VMEM((2, 128, 128), F32),
            VMEM((128, 128), F32),
            VMEM((*halves, 2, 4, 128, 128), F32),
            VMEM((*halves, 2, 4, 128, 128), F32),
            VMEM((*halves, 8, 128, 128), F32),
            VMEM((*halves, 8, 128, 128), F32),
            VMEM((4096, 128), F32),
            VMEM((128, 128), F32),
            VMEM((2, 8, 8, 256), F32),
            VMEM((8, 8, 256), F32),
            VMEM((8, 8, 256), F32),
            VMEM((8, 8, 256), F32),
            VMEM((2, 128, 128), F32),
            dma((16,)),
            dma((*halves, 12, CHUNKS)), dma((*halves, 8, CHUNKS)),
            dma((*halves, 2)), dma((*halves, 2)),
            dma((*halves, 8, CHUNKS)), dma((*halves, 8, CHUNKS)),
            dma, dma,
            dma((8,)), dma((8,)),
        ],
        compiler_params=pltpu.CompilerParams(
            collective_id=0, has_side_effects=True, vmem_limit_bytes=58 * 2**20
        ),
        cost_estimate=pl.CostEstimate(
            flops=3 * 2 * 4096 * 2048 * 256, bytes_accessed=17 * 2**20, transcendentals=3 * 32768
        ),
    )(source, value, occupancy.T, exponent.T)


def solution(mesh):
    placed = (P(("row", "col"), None), P("row", "col"), P("row", "col"), P("row", "col"))
    return jax.shard_map(
        shards, mesh=mesh, in_specs=placed, out_specs=P(("row", "col"), None), check_vma=False
    )
```

```python
import jax
import jax.numpy as jnp
from jax import lax
from jax.experimental import pallas as pl
from jax.experimental.pallas import tpu as pltpu
from jax.sharding import PartitionSpec as P

STEPS = 3
EPSILON = 1e-05
RETAIN = 0.8
TELEPORT = 0.2
NODES = 32768
FORWARDED = (1, 3, 2)
AHEAD = 6
CHUNKS = 2
CHUNK = 128 // CHUNKS
F32, BF16 = jnp.float32, jnp.bfloat16
MESH = pl.DeviceIdType.MESH
VMEM = pltpu.VMEM


def low_lanes(rows=128):
    return lax.broadcasted_iota(jnp.int32, (rows, 128), 1) < 64


def fold(top, bottom):
    low = low_lanes(top.shape[0])
    return jnp.where(low, top, bottom) + pltpu.roll(jnp.where(low, bottom, top), 64, 1)


def kernel(
    src_hbm, val_ref, occ_hbm, exp_hbm, out_ref,
    src_ref, occ_ref, exp_ref, small_sem,
    stage_ref, a_ref, scale_ref, x_ref, rhs_ref, acc_ref, psrc_ref, inv_ref,
    core_out, core_in, col_out, col_in,
    squares, tall, e_part, e_core, e_out, e_in, last_ref,
    load_sem, ag_ss, ag_rs, core_ss, core_rs, col_ss, col_rs,
    ec_ss, ec_rs, e_ss, e_rs,
):
    row, col = lax.axis_index("row"), lax.axis_index("col")
    yh, x = row // 4, row % 4
    z, yl, core = col // 4, (col // 2) % 2, col % 2
    sibling = (row, z * 4 + yl * 2 + 1 - core)

    def load(place):
        owner = place % 8 * 2 + place // 8
        return pltpu.make_async_copy(
            val_ref.at[pl.ds(pl.multiple_of(owner * 256, 256), 256)],
            stage_ref.at[place % AHEAD],
            load_sem.at[place],
        )

    small = [
        pltpu.make_async_copy(there, here, small_sem.at[k])
        for k, (there, here) in enumerate(
            [(src_hbm, src_ref), (occ_hbm, occ_ref), (exp_hbm, exp_ref)]
        )
    ]
    for copy in small:
        copy.start()

    row_mates = []
    for dy in (0, 1):
        for dx in (1, 3, 2, 0):
            if dx or dy:
                row_mates.append((((yh + dy) % 2) * 4 + (x + dx) % 4, col))
    col_mates = []
    for dz in (2, 1, 3, 0):
        for dy in (1, 0):
            if dz or dy:
                zz, yy = (z + dz) % 4, (yl + dy) % 2
                col_mates.append((zz * 2 + yy, (row, zz * 4 + yy * 2 + core)))

    barrier = pltpu.get_barrier_semaphore()
    mates = row_mates + [m for _, m in col_mates] + [sibling]
    for mate in mates:
        pl.semaphore_signal(barrier, inc=1, device_id=mate, device_id_type=MESH)

    for place in range(AHEAD):
        load(place).start()
    low = low_lanes()
    small[0].wait()
    top, bottom = src_ref[0:128], src_ref[128:256]
    packed = (
        jnp.where(low, top, pltpu.roll(bottom, 64, 1)),
        jnp.where(low, pltpu.roll(top, 64, 1), bottom),
    )
    for h in range(2):
        psrc_ref[h] = packed[h]
        x_ref[0, h, row] = packed[h]
    pl.semaphore_wait(barrier, len(mates))

    partner = (1 - yh) * 4 + x

    def rows_of(k):
        return pl.ds(k * CHUNK, CHUNK)

    def gather_copy(s, h, a, k, send, mate):
        return pltpu.make_async_remote_copy(
            x_ref.at[s, h, a, rows_of(k)], x_ref.at[s, h, a, rows_of(k)],
            ag_ss.at[s, h, send, k], ag_rs.at[s, h, a, k],
            device_id=(mate, col), device_id_type=MESH,
        )

    def spread(s, h, k):
        mates = [partner] + [yh * 4 + (x + dx) % 4 for dx in (1, 3, 2)]
        mates += [(1 - yh) * 4 + (x + dx) % 4 for dx in (2, 1, 3) if (s, h) == (0, 0) or dx not in FORWARDED]
        return [gather_copy(s, h, row, k, mate, mate) for mate in mates]

    def forward(s, h, k):
        if (s, h) == (0, 0):
            return []
        return [
            gather_copy(s, h, partner, k, 8 + dx, yh * 4 + (x + dx) % 4) for dx in FORWARDED
        ]

    def arrive(s, h, a):
        for k in range(CHUNKS):
            gather_copy(s, h, a, k, a, a).wait_recv()

    def pass_on(s, h):
        for k in range(CHUNKS):
            gather_copy(s, h, partner, k, partner, partner).wait_recv()
            for copy in forward(s, h, k):
                copy.start()

    def to_sibling(s, h, pair):
        return pltpu.make_async_remote_copy(
            core_out.at[s, h, pair], core_in.at[s, h, pair],
            core_ss.at[s, h, pair], core_rs.at[s, h, pair],
            device_id=sibling, device_id_type=MESH,
        )

    def to_owner(s, h, zz, yy, k):
        return pltpu.make_async_remote_copy(
            col_out.at[s, h, zz * 2 + yy, rows_of(k)], col_in.at[s, h, z * 2 + yl, rows_of(k)],
            col_ss.at[s, h, zz * 2 + yy, k], col_rs.at[s, h, z * 2 + yl, k],
            device_id=(row, zz * 4 + yy * 2 + core), device_id_type=MESH,
        )

    def from_mate(s, h, slot, mate, k):
        return pltpu.make_async_remote_copy(
            col_out.at[s, h, slot, rows_of(k)], col_in.at[s, h, slot, rows_of(k)],
            col_ss.at[s, h, slot, k], col_rs.at[s, h, slot, k],
            device_id=mate, device_id_type=MESH,
        )

    for k in range(CHUNKS):
        for copy in spread(0, 0, k):
            copy.start()

    small[1].wait()
    small[2].wait()
    tall[...] = jnp.zeros_like(tall)
    tall[0:16, 0:32] = occ_ref[...].astype(F32) * (
        (jnp.int32(1) << (exp_ref[...] + 3)).astype(F32) * 0.125
    )
    scale = jnp.transpose(tall[...])
    for j in range(16):
        across = jnp.broadcast_to(scale[0:32, j : j + 1], (32, 128))
        for i in range(32):
            scale_ref[i, :, j * 128 : (j + 1) * 128] = jnp.broadcast_to(
                across[i : i + 1], (16, 128)
            ).astype(BF16)

    squares[0:256, :] = jnp.zeros((256, 128), F32)

    def sum_lanes(place):
        ones = jnp.ones((8, 128), BF16)
        dims = (((1,), (1,)), ((), ()))
        part = squares[pl.ds(pl.multiple_of(place * 256, 256), 256), :]
        high = part.astype(BF16)
        rest = (part - high.astype(F32)).astype(BF16)
        e_part[place // 8, place % 8] = lax.dot_general(
            ones, high, dims, preferred_element_type=F32
        ) + lax.dot_general(ones, rest, dims, preferred_element_type=F32)

    def base_of(a):
        return ((a // 4 + yh) % 2 * 4 + (a % 4 + 4 - x) % 4) * 256

    bases = [base_of(a) for a in range(8)]

    def scale_rows(place, _):
        load(place).wait()
        owner = place % 8 * 2 + place // 8
        slot = place % AHEAD
        sum_lanes(jnp.maximum(place - 1, 0))
        for half in range(2):
            base = pl.multiple_of(place * 256 + half * 128, 128)
            for q in range(4):
                total = [jnp.zeros((16, 128), F32)] * 2
                rows = [pl.ds(half * 128 + q * 32 + r * 16, 16) for r in range(2)]
                out_rows = [pl.ds(base + q * 32 + r * 16, 16) for r in range(2)]
                for j in range(16):
                    lanes = slice(j * 128, (j + 1) * 128)
                    out_lanes = pl.ds(pl.multiple_of(bases[j // 2] + j % 2 * 128, 128), 128)
                    factor = scale_ref[owner * 2 + half, :, lanes]
                    for r in range(2):
                        part = stage_ref[slot, rows[r], lanes] * factor
                        a_ref[out_rows[r], out_lanes] = part
                        wide = part.astype(F32)
                        total[r] = total[r] + wide * wide
                for r in range(2):
                    squares[out_rows[r], :] = total[r]

        @pl.when(place < 16 - AHEAD)
        def _():
            load(place + AHEAD).start()

        return 0

    lax.fori_loop(0, 16, scale_rows, 0)
    sum_lanes(15)
    for k in range(CHUNKS):
        for copy in spread(0, 1, k):
            copy.start()

    e_sib = pltpu.make_async_remote_copy(
        e_part.at[1 - core], e_core, ec_ss, ec_rs, device_id=sibling, device_id_type=MESH
    )

    def e_mate(slot, mate, there):
        return pltpu.make_async_remote_copy(
            e_out.at[slot], e_in.at[there], e_ss.at[slot], e_rs.at[there],
            device_id=mate, device_id_type=MESH,
        )

    def send_energy():
        e_sib.wait()
        e_out[...] = e_part[core] + e_core[...]
        for slot, mate in col_mates:
            e_mate(slot, mate, z * 2 + yl).start()

    def take_energy():
        energy = e_out[z * 2 + yl]
        for slot, mate in col_mates:
            e_mate(slot, mate, slot).wait_recv()
            energy = energy + e_in[slot]
        across = [
            jnp.transpose(jnp.broadcast_to(energy[0:1, k * 128 : (k + 1) * 128], (128, 128)))
            for k in range(2)
        ]
        mean = jnp.where(low, across[0], across[1]) / NODES
        inv_ref[...] = 1.0 / (jnp.sqrt(NODES * 1.0) * jnp.sqrt(mean + EPSILON))

    def load_rhs(s, h, a):
        part = x_ref[s, h, a]
        high = part.astype(BF16).astype(F32)
        rest = pltpu.roll(part - high, 64, 1)
        base = pl.multiple_of(base_of(a), 256)
        rhs_ref[pl.ds(base, 128), :] = jnp.where(low, high, rest).astype(BF16)
        rhs_ref[pl.ds(base + 128, 128), :] = jnp.where(low, rest, high).astype(BF16)

    def multiply_near(s, h):
        load_rhs(s, h, row)
        load_rhs(s, h, partner)
        for dx in (1, 3, 2):
            a = yh * 4 + (x + dx) % 4
            arrive(s, h, a)
            load_rhs(s, h, a)

        def tile(m, _):
            rows = pl.ds(pl.multiple_of(m * 2048, 2048), 2048)
            acc_ref[rows, :] = jnp.dot(
                a_ref[rows, 0:1280], rhs_ref[0:1280, :],
                preferred_element_type=F32,
            )
            return 0

        lax.fori_loop(0, 2, tile, 0)

    def far_tile(whose, pair):
        rows = pl.ds(pl.multiple_of(whose * 2048 + pair * 1024, 1024), 1024)
        total = acc_ref[rows, :] + jnp.dot(
            a_ref[rows, 1280:2048], rhs_ref[1280:2048, :],
            preferred_element_type=F32,
        )
        return [fold(total[b * 256 : b * 256 + 128], total[b * 256 + 128 : b * 256 + 256]) for b in range(4)]

    def multiply_far(s, h):
        for dx in (1, 3, 2):
            a = (1 - yh) * 4 + (x + dx) % 4
            arrive(s, h, a)
            load_rhs(s, h, a)

        def theirs(it, _):
            pair = (z // 2 + 1 + it) % 2
            blocks = far_tile(1 - core, pair)
            for b in range(4):
                core_out[s, h, pair, b] = blocks[b]
            to_sibling(s, h, pair).start()
            return 0

        lax.fori_loop(0, 2, theirs, 0)

    def join(s, h):
        def mine(it, _):
            pair = (z // 2 + 1 + it) % 2
            blocks = far_tile(core, pair)
            to_sibling(s, h, pair).wait_recv()
            for b in range(4):
                col_out[s, h, pair * 4 + b] = blocks[b] + core_in[s, h, pair, b]

            @pl.when(it == 0)
            def _():
                for b in range(4):
                    to_owner(s, h, pair * 2 + b // 2, b % 2, 0).start()

            return 0

        lax.fori_loop(0, 2, mine, 0)
        last = [(z // 2 * 2 + (z + 1) % 2, 1 - yl), (z // 2 * 2 + (z + 1) % 2, yl), (z, 1 - yl)]
        first = [((z // 2 * 2 + 2 + b // 2) % 4, b % 2) for b in range(4)]
        for zz, yy in last:
            to_owner(s, h, zz, yy, 0).start()
        for k in range(1, CHUNKS):
            for zz, yy in first + last:
                to_owner(s, h, zz, yy, k).start()

    def finish(s, h, k):
        rows = rows_of(k)
        total = col_out[s, h, z * 2 + yl, rows]
        for slot, mate in col_mates:
            from_mate(s, h, slot, mate, k).wait_recv()
            total = total + col_in[s, h, slot, rows]
        new = jnp.tanh(RETAIN * total * inv_ref[rows] + TELEPORT * psrc_ref[h, rows])
        if s < STEPS - 1:
            x_ref[s + 1, h, row, rows] = new
            for copy in spread(s + 1, h, k):
                copy.start()
        else:
            last_ref[h, rows] = new

    pass_on(0, 0)
    e_sib.start()
    multiply_near(0, 0)
    send_energy()
    multiply_far(0, 0)
    join(0, 0)
    for s in range(STEPS):
        pass_on(s, 1)
        multiply_near(s, 1)
        if s == 0:
            take_energy()
        if s < STEPS - 1:
            finish(s, 0, 0)
            multiply_far(s, 1)
            finish(s, 0, 1)
            join(s, 1)
            pass_on(s + 1, 0)
            multiply_near(s + 1, 0)
            finish(s, 1, 0)
            multiply_far(s + 1, 0)
            finish(s, 1, 1)
            join(s + 1, 0)
        else:
            multiply_far(s, 1)
            join(s, 1)
            for h in range(2):
                for k in range(CHUNKS):
                    finish(s, h, k)

    left, right = last_ref[0], last_ref[1]
    out_ref[0:128] = jnp.where(low, left, pltpu.roll(right, 64, 1))
    out_ref[128:256] = jnp.where(low, pltpu.roll(left, 64, 1), right)

    for slot, mate in col_mates:
        e_mate(slot, mate, slot).wait_send()
    for s in range(STEPS):
        for h in range(2):
            for k in range(CHUNKS):
                for copy in spread(s, h, k) + forward(s, h, k):
                    copy.wait_send()
            for pair in range(2):
                to_sibling(s, h, pair).wait_send()
            for slot, mate in col_mates:
                for k in range(CHUNKS):
                    from_mate(s, h, slot, mate, k).wait_send()


def shards(source, value, occupancy, exponent):
    vmem = pl.BlockSpec(memory_space=VMEM)
    dma = pltpu.SemaphoreType.DMA
    halves = (STEPS, 2)
    return pl.pallas_call(
        kernel,
        out_shape=pltpu.VMEM((256, 128), F32),
        in_specs=[pl.BlockSpec(memory_space=pltpu.HBM)] * 4,
        out_specs=vmem,
        scratch_shapes=[
            VMEM((256, 128), F32),
            VMEM((16, 32), jnp.int32),
            VMEM((16, 32), jnp.int32),
            dma((3,)),
            VMEM((AHEAD, 256, 2048), BF16),
            VMEM((4096, 2048), BF16),
            VMEM((32, 16, 2048), BF16),
            VMEM((*halves, 8, 128, 128), F32),
            VMEM((2048, 128), BF16),
            VMEM((4096, 128), F32),
            VMEM((2, 128, 128), F32),
            VMEM((128, 128), F32),
            VMEM((*halves, 2, 4, 128, 128), F32),
            VMEM((*halves, 2, 4, 128, 128), F32),
            VMEM((*halves, 8, 128, 128), F32),
            VMEM((*halves, 8, 128, 128), F32),
            VMEM((4096, 128), F32),
            VMEM((128, 128), F32),
            VMEM((2, 8, 8, 256), F32),
            VMEM((8, 8, 256), F32),
            VMEM((8, 8, 256), F32),
            VMEM((8, 8, 256), F32),
            VMEM((2, 128, 128), F32),
            dma((16,)),
            dma((*halves, 12, CHUNKS)), dma((*halves, 8, CHUNKS)),
            dma((*halves, 2)), dma((*halves, 2)),
            dma((*halves, 8, CHUNKS)), dma((*halves, 8, CHUNKS)),
            dma, dma,
            dma((8,)), dma((8,)),
        ],
        compiler_params=pltpu.CompilerParams(
            collective_id=0, has_side_effects=True, vmem_limit_bytes=58 * 2**20
        ),
        cost_estimate=pl.CostEstimate(
            flops=3 * 2 * 4096 * 2048 * 256, bytes_accessed=17 * 2**20, transcendentals=3 * 32768
        ),
    )(source, value, occupancy.T, exponent.T)


def solution(mesh):
    placed = (P(("row", "col"), None), P("row", "col"), P("row", "col"), P("row", "col"))
    return jax.shard_map(
        shards, mesh=mesh, in_specs=placed, out_specs=P(("row", "col"), None), check_vma=False
    )
```
